32 devices in a mesh: role: 2 (over core), dp: 4 (over y, x), tensor: 4 (over z).
Axes of the slice: x: 2, y: 2, z: 4, core: 2. Of those that a mesh axis runs over, the one named last changes fastest.
Arguments:
- queries: bfloat16 [128, 128, 576], P(('dp', 'tensor'), 'role'), may hold values from -13 to 13
- latent_cache: bfloat16 [64, 1024, 576], P(('dp', 'tensor')), may hold values from -4 to 4
- new_latent: bfloat16 [128, 576], P(('dp', 'tensor')), may hold values from -9 to 9
- cache_lengths: int32 [64], P(('dp', 'tensor')), may hold values from 2 to 1024
- value_proj: bfloat16 [128, 512, 128], P(('role', 'tensor')), may hold values from -1 to 1
- out_proj: bfloat16 [16384, 7168], P(('role', 'tensor'), 'dp'), may hold values from -0.046875 to 0.046875
- residual: bfloat16 [128, 7168], P(('role', 'tensor'), 'dp'), may hold values from -68 to 68
- norm_gain: bfloat16 [7168], replicated, may hold values from 0.5 to 1.5
- routes: int32 [128, 8], P(('role', 'tensor')), may hold values from 0 to 15, all different within a row; in each aligned block of 16 rows (0 to 15, 16 to 31, ...) at most 10 rows name the same one
- gate_values: float32 [128, 8], P(('role', 'tensor')), may hold values from 0.2 to 0.8
- tenant_ids: int32 [128], P(('role', 'tensor')), may hold values from 0 to 2
- expert_gate_weight: bfloat16 [16, 7168, 2048], P('dp', None, ('role', 'tensor')), may hold values from -0.0625 to 0.0625
- expert_up_weight: bfloat16 [16, 7168, 2048], P('dp', None, ('role', 'tensor')), may hold values from -0.0625 to 0.0625
- expert_down_weight: bfloat16 [16, 2048, 7168], P('dp', ('role', 'tensor')), may hold values from -0.125 to 0.125
- left_delta_factor: bfloat16 [3, 16, 2048, 64], P(None, 'dp', ('role', 'tensor')), may hold values from -0.125 to 0.125
- factor_right: bfloat16 [3, 16, 64, 7168], P(None, 'dp'), may hold values from -0.75 to 0.75
Outputs:
- mixed: bfloat16 [128, 7168], P(('role', 'tensor'), 'dp')
The draws below stay inside these ranges and needn't reach their ends.
Inputs may be any that keep to these rules, and one draw needn't show every extreme that they name: `routes`: in each aligned block of 16 tokens no expert is named by more than 10 of them.
All inputs are finite; a program needn't handle non-finite values.
Results may differ from the reference program's by a relative error of at most 0.008.
Values may be sent and summed in bfloat16 or wider, within the bound.
A program may use at most 128 MiB of HBM per device.

```python
import math
import jax
import jax.numpy as jnp
import numpy as np
from jax import lax

D = 7168
H = 128
LAT = 512
ROPE = 64
VH = 128
FF = 2048
TOP = 8
EXPERTS = 16
RANK = 64
TEN = 3
CTX = 1024
SEQS = 64
TOKENS = 128
TOK_GRP = 16
CAP = 10


def draw_latent_cache(key, part):
    width = LAT + ROPE
    values = jnp.clip(jax.random.normal(jax.random.fold_in(key, 1), (SEQS, CTX, width), jnp.float32), -4.0, 4.0)
    return values.astype(jnp.bfloat16)


def draw_queries(key, part):
    width = LAT + ROPE
    values = jnp.clip(jax.random.normal(jax.random.fold_in(key, 2), (TOKENS, H, width), jnp.float32), -4.0, 4.0)
    return values.astype(jnp.bfloat16)


def draw_residual(key, part):
    noise = jnp.clip(jax.random.normal(jax.random.fold_in(key, 3), (TOKENS, D), jnp.float32), -4.0, 4.0)
    column = jnp.arange(D, dtype=jnp.float32) / D
    row_scale = jnp.exp(jax.random.uniform(jax.random.fold_in(key, 4), (TOKENS, 1), jnp.float32, math.log(0.3), math.log(3.0)))
    col_scale = 0.3 * jnp.exp(column * math.log(10.0))
    values = noise * row_scale * col_scale[None, :]
    return values.astype(jnp.bfloat16)


def draw_cache_lengths(key, part):
    drawn = jax.random.randint(jax.random.fold_in(key, 5), (SEQS,), 2, CTX + 1, dtype=jnp.int32)
    offset = jax.random.randint(jax.random.fold_in(key, 6), (), 0, 4, dtype=jnp.int32)
    full = jnp.arange(SEQS, dtype=jnp.int32) % 4 == offset
    return jnp.where(full, CTX, drawn).astype(jnp.int32)


def plant(entries, own_key, low, high):
    spot = [jax.random.randint(jax.random.fold_in(own_key, axis), (), 0, length) for axis, length in enumerate(entries.shape)]
    longest = entries.shape.index(max(entries.shape))
    beside = spot[:longest] + [(spot[longest] + 1) % entries.shape[longest]] + spot[longest + 1:]
    return entries.at[tuple(spot)].set(low).at[tuple(beside)].set(high)


def levels(key, dims, pieces, smallest, largest):
    gain = 1.0
    for axis_at, parts in pieces:
        draws = jax.random.uniform(jax.random.fold_in(jax.random.fold_in(key, 6), axis_at), (parts,), jnp.float32, smallest / len(pieces), largest / len(pieces))
        gain = gain * jnp.repeat(jnp.exp(draws), dims[axis_at] // parts).reshape((-1,) + (1,) * (len(dims) - 1 - axis_at))
    return gain


def assign_block(key, own, number, rows, count, top, bound, slope):
    ranking = jax.random.permutation(key, count)
    crowded, usual = shares(count, rows * top, bound, slope, True), shares(count, rows * top, bound, slope, False)
    places = jnp.arange(count)

    def named(sizes, offset_by):
        used = int((sizes > 0).sum())
        fixed = max(1, used // 4)
        shifted = fixed + (places - fixed + offset_by * (used - fixed)) % max(1, count - fixed)
        return jnp.zeros((count,), jnp.int32).at[ranking[jnp.where(places < fixed, places, shifted)]].set(jnp.asarray(sizes, jnp.int32))

    sizes = jnp.where(number % 4 == 0, named(crowded, number // 4), named(usual, number - number // 4 - 1))
    mixed = jax.random.permutation(jax.random.fold_in(own, 3), count)
    source_of, sink = mixed[0:count // 2 * 2:2], mixed[1:count // 2 * 2:2]
    slack = jnp.minimum(sizes[source_of] - 1, bound - sizes[sink]) // 2
    slack = jnp.where((source_of == ranking[0]) | (sink == ranking[0]) | (sizes[sink] == 0), 0, jnp.maximum(slack, 0))
    shifted = jax.random.randint(jax.random.fold_in(own, 4), (count // 2,), 0, 1 << 20) % (slack + 1)
    sizes = sizes.at[source_of].add(-shifted).at[sink].add(shifted)
    members = jnp.searchsorted(jnp.cumsum(sizes), jnp.arange(rows * top), side="right").astype(jnp.int32)
    table = members.reshape(top, rows).T
    table = table[jax.random.permutation(jax.random.fold_in(own, 1), rows)]
    offset_by = jax.random.randint(jax.random.fold_in(own, 2), (rows, 1), 0, top)
    return jnp.take_along_axis(table, (jnp.arange(top)[None, :] + offset_by) % top, axis=1)


def shares(number_of, total, most, lean, full):
    weights = [(1 << 20) // math.isqrt(standing ** lean) + 1 for standing in range(1, number_of + 1)]
    largest = most if full else min(most, max(-(-total // number_of), total * weights[0] // sum(weights)))
    least = 1 if total - largest >= number_of - 1 else 0
    given, spare = [largest] + [least] * (number_of - 1), total - largest - least * (number_of - 1)
    while spare > 0:
        candidates = [i for i in range(1, number_of) if given[i] < largest] or [i for i in range(1, number_of) if given[i] < most]
        pool, left = sum([weights[i] for i in candidates]), spare
        for i in candidates:
            addition = min(most - given[i], max(1, left * weights[i] // pool), spare)
            given[i] = given[i] + addition
            spare = spare - addition
    return np.array(given)


def bell_draw(stream_key, extent, deviation, most, shards=(), kind=jnp.bfloat16):
    values = jax.random.normal(stream_key, extent, jnp.float32) * deviation
    if len(shards) > 0:
        values = levels(stream_key, extent, shards, -0.22, 0.18) * values
    return jnp.clip(values, min=-most, max=most).astype(kind)


def setup_inputs(seed: int = 0) -> dict:
    arg_keys = jax.random.split(jax.random.key(seed), 17)
    queries = draw_queries(jax.random.fold_in(arg_keys[16], 71), 0)
    latent_cache = draw_latent_cache(jax.random.fold_in(arg_keys[16], 71), 0)
    new_latent = bell_draw(arg_keys[2], (TOKENS, LAT + ROPE), 2.2, 9.0, ((0, 16),))
    cache_lengths = draw_cache_lengths(jax.random.fold_in(arg_keys[16], 71), 0)
    value_proj = bell_draw(arg_keys[4], (H, LAT, VH), (max(LAT // 16, 1)) ** -0.5, 1.0, ((0, 8),))
    out_proj = bell_draw(arg_keys[5], (H * VH, D), (H * VH) ** -0.5, 0.046875, ((0, 8), (1, 4)))
    residual = draw_residual(jax.random.fold_in(arg_keys[16], 71), 0)
    norm_gain = jnp.clip(1.0 + 0.1 * jax.random.normal(arg_keys[7], (D,), jnp.float32), 0.5, 1.5).astype(jnp.bfloat16)
    routes_keys = jax.random.split(jax.random.fold_in(arg_keys[8], 1), TOKENS // TOK_GRP)
    routes_turns = jax.random.permutation(jax.random.fold_in(arg_keys[8], 3), TOKENS // TOK_GRP)
    routes = jax.vmap(lambda own, number: assign_block(jax.random.fold_in(arg_keys[8], 2), own, number, TOK_GRP, EXPERTS, TOP, CAP, 2))(routes_keys, routes_turns).reshape((TOKENS, TOP))
    gate_values = jnp.clip(0.2 + 0.6 * jax.random.uniform(arg_keys[9], (TOKENS, TOP), jnp.float32) ** levels(arg_keys[9], (TOKENS, TOP), ((0, 8),), -0.2, 0.2), 0.2, 0.8)
    tenant_ids = plant(jax.random.randint(arg_keys[10], (TOKENS,), 0, TEN), jax.random.fold_in(arg_keys[10], 1), 0, TEN - 1).astype(jnp.int32)
    expert_gate_weight = bell_draw(arg_keys[11], (EXPERTS, D, FF), D ** -0.5, 0.0625, ((0, 4), (2, 8)))
    expert_up_weight = bell_draw(arg_keys[12], (EXPERTS, D, FF), D ** -0.5, 0.0625, ((0, 4), (2, 8)))
    expert_down_weight = bell_draw(arg_keys[13], (EXPERTS, FF, D), FF ** -0.5, 0.125, ((0, 4), (1, 8)))
    left_delta_factor = bell_draw(arg_keys[14], (TEN, EXPERTS, FF, RANK), FF ** -0.5, 0.125, ((1, 4), (2, 8)))
    factor_right = bell_draw(arg_keys[15], (TEN, EXPERTS, RANK, D), RANK ** -0.5, 0.75, ((1, 4),))
    return dict(queries=queries, latent_cache=latent_cache, new_latent=new_latent, cache_lengths=cache_lengths, value_proj=value_proj, out_proj=out_proj, residual=residual, norm_gain=norm_gain, routes=routes, gate_values=gate_values, tenant_ids=tenant_ids, expert_gate_weight=expert_gate_weight, expert_up_weight=expert_up_weight, expert_down_weight=expert_down_weight, left_delta_factor=left_delta_factor, factor_right=factor_right)


SCORE_SCALE = 0.07216878364870323
NORM_EPS = 1e-06

def attend_sequence(inputs):
    query_pair, cache_rows, fresh_rows, length = inputs
    keys = jnp.concatenate([cache_rows, fresh_rows], axis=0).astype(jnp.float32)
    scores = jnp.einsum('qhd,pd->qhp', query_pair.astype(jnp.float32), keys, precision=lax.Precision.HIGHEST) * SCORE_SCALE
    cached = jnp.arange(CTX, dtype=jnp.int32) < length
    cached = jnp.broadcast_to(cached[None, :], (2, CTX))
    causal = jnp.arange(2, dtype=jnp.int32)[:, None] >= jnp.arange(2, dtype=jnp.int32)[None, :]
    valid = jnp.concatenate([cached, causal], axis=1)
    scores = jnp.where(valid[:, None, :], scores, -jnp.inf)
    top = lax.optimization_barrier(jnp.max(scores, axis=2, keepdims=True))
    weights = jnp.exp(scores - top)
    total = lax.optimization_barrier(jnp.sum(weights, axis=2))
    rounded = lax.optimization_barrier(weights.astype(jnp.bfloat16)).astype(jnp.float32)
    summed = jnp.einsum('qhp,pd->qhd', rounded, keys[:, :LAT], precision=lax.Precision.HIGHEST)
    return (summed / total[..., None]).astype(jnp.bfloat16)

def reference(queries, latent_cache, new_latent, cache_lengths, value_proj, out_proj, residual, norm_gain, routes, gate_values, tenant_ids, expert_gate_weight, expert_up_weight, expert_down_weight, left_delta_factor, factor_right):
    width = LAT + ROPE
    attended = lax.map(attend_sequence, (queries.reshape(SEQS, 2, H, width), latent_cache, new_latent.reshape(SEQS, 2, width), cache_lengths))
    attended = attended.reshape(TOKENS, H, LAT)
    head_values = jnp.einsum('thl,hlv->thv', attended.astype(jnp.float32), value_proj.astype(jnp.float32), precision=lax.Precision.HIGHEST).astype(jnp.bfloat16)
    attention = jnp.dot(head_values.reshape(TOKENS, H * VH), out_proj, preferred_element_type=jnp.float32)
    mixed_in = lax.optimization_barrier((residual.astype(jnp.float32) + attention).astype(jnp.bfloat16))
    wide = mixed_in.astype(jnp.float32)
    scale = lax.rsqrt(lax.optimization_barrier(jnp.mean(wide * wide, axis=1, keepdims=True)) + NORM_EPS)
    normed = (wide * scale * norm_gain.astype(jnp.float32)[None, :]).astype(jnp.bfloat16)
    groups = TOKENS // TOK_GRP
    route_groups = routes.reshape(groups, TOK_GRP, TOP)
    labels = jnp.arange(EXPERTS, dtype=jnp.int32)
    chosen = (route_groups[..., None] == labels[None, None, None, :]).astype(jnp.int32)
    routed = lax.optimization_barrier(jnp.sum(chosen, axis=2)).astype(jnp.int32)
    earlier = (jnp.cumsum(routed, axis=1) - routed).astype(jnp.int32)
    slot_ids = jnp.arange(CAP, dtype=jnp.int32)
    routed_t = jnp.transpose(routed, (2, 0, 1))
    earlier_t = jnp.transpose(earlier, (2, 0, 1))
    table = (routed_t[:, :, None, :] > 0) & (earlier_t[:, :, None, :] == slot_ids[None, None, :, None])
    normed_groups = normed.reshape(groups, TOK_GRP, D).astype(jnp.float32)
    tenant_groups = tenant_ids.reshape(groups, TOK_GRP).astype(jnp.int32)
    tenant_labels = jnp.arange(TEN, dtype=jnp.int32)

    def run_expert(inputs):
        choose, gate_w, up_w, down_w, left_w, right_w = inputs
        input_rows = jnp.einsum('ncg,ngd->ncd', choose.astype(jnp.float32), normed_groups, precision=lax.Precision.HIGHEST)
        input_rows = input_rows.astype(jnp.bfloat16).reshape(groups * CAP, D)
        owners = lax.optimization_barrier(jnp.sum(choose.astype(jnp.int32) * tenant_groups[:, None, :], axis=2)).astype(jnp.int32).reshape(groups * CAP)
        gate_scores = jnp.dot(input_rows, gate_w, preferred_element_type=jnp.float32)
        upper_bound = jnp.dot(input_rows, up_w, preferred_element_type=jnp.float32)
        hidden = (jax.nn.silu(gate_scores) * upper_bound).astype(jnp.bfloat16)
        base_output = jnp.dot(hidden, down_w, preferred_element_type=jnp.float32)
        owner_mask = (owners[:, None] == tenant_labels[None, :]).astype(jnp.float32)
        mixing_coefficient = jnp.einsum('sf,tfr->str', hidden.astype(jnp.float32), left_w.astype(jnp.float32), precision=lax.Precision.HIGHEST)
        mixing_coefficient = mixing_coefficient * owner_mask[:, :, None]
        delta = jnp.einsum('str,trd->sd', mixing_coefficient, right_w.astype(jnp.float32), precision=lax.Precision.HIGHEST)
        return (base_output - delta).astype(jnp.bfloat16).reshape(groups, CAP, D)
    outputs = lax.map(run_expert, (table, expert_gate_weight, expert_up_weight, expert_down_weight, jnp.transpose(left_delta_factor, (1, 0, 2, 3)), jnp.transpose(factor_right, (1, 0, 2, 3))))
    gate_of = lax.optimization_barrier(jnp.sum(gate_values.reshape(groups, TOK_GRP, TOP)[..., None] * chosen.astype(jnp.float32), axis=2))
    weighting = table.astype(jnp.float32) * jnp.transpose(gate_of, (2, 0, 1))[:, :, None, :]
    expert_part = jnp.einsum('encg,encd->ngd', weighting, outputs.astype(jnp.float32), precision=lax.Precision.HIGHEST)
    return (wide + expert_part.reshape(TOKENS, D)).astype(jnp.bfloat16)
```

```python
import jax
import jax.numpy as jnp
from jax import lax
from jax.sharding import PartitionSpec as P

LAT = 512
EXPERTS = 16
TEN = 3


SCORE_SCALE = 0.07216878364870323
NORM_EPS = 1e-06
MASKED = -1e30


def rms_rows(input_rows, norm_gain):
    wide = input_rows.astype(jnp.float32)
    scale = lax.rsqrt(jnp.mean(wide * wide, axis=-1, keepdims=True) + NORM_EPS)
    return (wide * scale * norm_gain.astype(jnp.float32)).astype(jnp.bfloat16)


def local(
    queries,
    latent_cache,
    new_latent,
    cache_lengths,
    value_proj,
    out_proj,
    residual,
    norm_gain,
    routes,
    gate_values,
    tenant_ids,
    expert_gate_weight,
    expert_up_weight,
    expert_down_weight,
    left_delta_factor,
    factor_right,
):
    seq_count, context, width = latent_cache.shape
    local_heads = queries.shape[1]
    paired = queries.reshape(seq_count, 2, local_heads, width)
    scores = (
        jnp.einsum("sqhd,spd->sqhp", paired, latent_cache, preferred_element_type=jnp.float32)
        * SCORE_SCALE
    )
    present = jnp.arange(context, dtype=jnp.int32)[None, :] < cache_lengths[:, None]
    scores = jnp.where(present[:, None, None, :], scores, MASKED)
    fresh_keys = new_latent.reshape(seq_count, 2, width)
    fresh = (
        jnp.einsum("sqhd,skd->sqhk", paired, fresh_keys, preferred_element_type=jnp.float32)
        * SCORE_SCALE
    )
    causal = jnp.arange(2)[:, None] >= jnp.arange(2)[None, :]
    fresh = jnp.where(causal[None, :, None, :], fresh, MASKED)
    top = jnp.maximum(jnp.max(scores, axis=3), jnp.max(fresh, axis=3))[..., None]
    weights = jnp.exp(scores - top)
    fresh_weights = jnp.exp(fresh - top)
    total = jnp.sum(weights, axis=3) + jnp.sum(fresh_weights, axis=3)
    summed = jnp.einsum(
        "sqhp,spd->sqhd",
        weights.astype(jnp.bfloat16),
        latent_cache[:, :, :LAT],
        preferred_element_type=jnp.float32,
    )
    summed = summed + jnp.einsum(
        "sqhk,skd->sqhd",
        fresh_weights.astype(jnp.bfloat16),
        fresh_keys[:, :, :LAT],
        preferred_element_type=jnp.float32,
    )
    attended = (
        (summed / total[..., None]).astype(jnp.bfloat16).reshape(seq_count * 2, local_heads, LAT)
    )
    by_head = lax.all_to_all(attended, "tensor", split_axis=1, concat_axis=0, tiled=True)
    head_values = jnp.einsum(
        "thl,hlv->thv", by_head, value_proj, preferred_element_type=jnp.float32
    ).astype(jnp.bfloat16)
    head_values = head_values.reshape(
        head_values.shape[0], head_values.shape[1] * head_values.shape[2]
    )
    all_values = lax.all_gather(head_values, "dp", axis=0, tiled=True)
    group_rows = residual.shape[0]
    input_rows = all_values
    attention = lax.psum_scatter(
        jnp.dot(input_rows, out_proj, preferred_element_type=jnp.float32),
        ("role", "tensor"),
        scatter_dimension=0,
        tiled=True,
    )
    mixed_in = lax.optimization_barrier(
        (residual.astype(jnp.float32) + attention).astype(jnp.bfloat16)
    )
    capacity = 5 * group_rows // 8
    labels = jnp.arange(EXPERTS, dtype=jnp.int32)
    chosen = (routes[:, :, None] == labels[None, None, :]).astype(jnp.int32)
    routed = jnp.sum(chosen, axis=1)
    rows_at = jnp.arange(group_rows, dtype=jnp.int32)
    before = (rows_at[:, None] > rows_at[None, :]).astype(jnp.int32)
    earlier = jnp.sum(before[:, :, None] * routed[None, :, :], axis=1)
    slot_ids = jnp.arange(capacity, dtype=jnp.int32)
    table = (routed.T[:, None, :] > 0) & (earlier.T[:, None, :] == slot_ids[None, :, None])
    local_experts = EXPERTS // lax.axis_size("dp")
    expert_start = lax.axis_index("dp") * local_experts
    mine = lax.dynamic_slice_in_dim(table, expert_start, local_experts, 0)
    full_rows = lax.all_gather(mixed_in, "dp", axis=1, tiled=True)
    picked = jnp.einsum(
        "ecg,gd->ecd", mine.astype(jnp.bfloat16), full_rows, preferred_element_type=jnp.float32
    ).astype(jnp.bfloat16)
    slot_rows = rms_rows(picked, norm_gain)
    slot_owner = jnp.sum(mine.astype(jnp.int32) * tenant_ids[None, None, :], axis=2)
    collected_rows, owners = (
        lax.all_gather(slot_rows, ("role", "tensor"), axis=1, tiled=True),
        lax.all_gather(slot_owner, ("role", "tensor"), axis=1, tiled=True),
    )
    gate_scores = jnp.einsum(
        "gpc,gcb->gpb", collected_rows, expert_gate_weight, preferred_element_type=jnp.float32
    )
    upper_bound = jnp.einsum(
        "gpc,gcb->gpb", collected_rows, expert_up_weight, preferred_element_type=jnp.float32
    )
    hidden = (jax.nn.silu(gate_scores) * upper_bound).astype(jnp.bfloat16)
    owner_mask = (owners[:, :, None] == jnp.arange(TEN, dtype=jnp.int32)[None, None, :]).astype(
        jnp.float32
    )
    widened_right_factor = factor_right.astype(jnp.float32)
    input_rows = hidden
    base_output = jnp.einsum(
        "xog,xgm->oxm", input_rows, expert_down_weight, preferred_element_type=jnp.float32
    )
    mixing_coefficient = (
        jnp.einsum(
            "ywv,oyvh->ywoh", input_rows, left_delta_factor, preferred_element_type=jnp.float32
        )
        * owner_mask[..., None]
    )
    outputs = lax.psum_scatter(
        base_output
        - jnp.einsum(
            "okei,eoiw->kow",
            mixing_coefficient,
            widened_right_factor,
            precision=lax.Precision.HIGHEST,
        ),
        ("role", "tensor"),
        scatter_dimension=0,
        tiled=True,
    ).astype(jnp.bfloat16)
    gate_of = jnp.sum(gate_values[:, :, None] * chosen.astype(jnp.float32), axis=1)
    weighting = table.astype(jnp.float32) * gate_of.T[:, None, :]
    own_weights = lax.dynamic_slice_in_dim(weighting, expert_start, local_experts, 0)
    token_terms = jnp.einsum(
        "lcg,cld->gd", own_weights, outputs.astype(jnp.float32), precision=lax.Precision.HIGHEST
    )
    expert_part = lax.psum_scatter(token_terms, "dp", scatter_dimension=1, tiled=True)
    return (mixed_in.astype(jnp.float32) + expert_part).astype(jnp.bfloat16)


def solution(mesh):
    placed = (
        P(("dp", "tensor"), "role", None),
        P(("dp", "tensor"), None, None),
        P(("dp", "tensor"), None),
        P(("dp", "tensor")),
        P(("role", "tensor"), None, None),
        P(("role", "tensor"), "dp"),
        P(("role", "tensor"), "dp"),
        P(),
        P(("role", "tensor"), None),
        P(("role", "tensor"), None),
        P(("role", "tensor")),
        P("dp", None, ("role", "tensor")),
        P("dp", None, ("role", "tensor")),
        P("dp", ("role", "tensor"), None),
        P(None, "dp", ("role", "tensor"), None),
        P(None, "dp", None, None),
    )
    return jax.shard_map(
        local, mesh=mesh, in_specs=placed, out_specs=P(("role", "tensor"), "dp"), check_vma=False
    )
```

```python
import functools
import jax
import jax.numpy as jnp
from jax import lax
from jax.experimental import pallas as pl
from jax.experimental.pallas import tpu as pltpu
from jax.sharding import PartitionSpec as P

LAT = 512
EXPERTS = 16
TEN = 3


SCORE_SCALE = 0.07216878364870323
NORM_EPS = 1e-06
MASKED = -1e30


MESH = pl.DeviceIdType.MESH
VMEM_BYTES = 56 * 1024 * 1024


def peer_of(axis, offset):
    size = lax.axis_size(axis)
    return lax.rem(lax.axis_index(axis) + offset, size)


def source_of(axis, offset):
    size = lax.axis_size(axis)
    return lax.rem(lax.axis_index(axis) + size - offset, size)


def greet(axes):
    barrier = pltpu.get_barrier_semaphore()
    count = 0
    for axis in axes:
        for offset in range(1, lax.axis_size(axis)):
            pl.semaphore_signal(
                barrier, inc=1, device_id={axis: peer_of(axis, offset)}, device_id_type=MESH
            )
            count += 1
    pl.semaphore_wait(barrier, count)


def remote(source, target, send, recv, axis, peer):
    return pltpu.make_async_remote_copy(
        src_ref=source,
        dst_ref=target,
        send_sem=send,
        recv_sem=recv,
        device_id={axis: peer},
        device_id_type=MESH,
    )


def exchange_kernel(axis, gather, block_ref, out_ref, send, recv, own_sem):
    size = lax.axis_size(axis)
    me = lax.axis_index(axis)
    own = pltpu.make_async_copy(
        block_ref if gather else block_ref.at[me], out_ref.at[me], own_sem
    )
    own.start()
    greet((axis,))
    copies = []
    for offset in range(1, size):
        peer = peer_of(axis, offset)
        copy = remote(
            block_ref if gather else block_ref.at[peer],
            out_ref.at[me],
            send.at[offset - 1],
            recv.at[offset - 1],
            axis,
            peer,
        )
        copy.start()
        copies.append(copy)
    own.wait()
    for copy in copies:
        copy.wait()


def exchange(blocks, axis, gather, collective_id):
    size = lax.axis_size(axis)
    shape = (size,) + blocks.shape if gather else blocks.shape
    return pl.pallas_call(
        functools.partial(exchange_kernel, axis, gather),
        out_shape=jax.ShapeDtypeStruct(shape, blocks.dtype),
        in_specs=[pl.BlockSpec(memory_space=pl.ANY)],
        out_specs=pl.BlockSpec(memory_space=pl.ANY),
        scratch_shapes=[
            pltpu.SemaphoreType.DMA((size - 1,)),
            pltpu.SemaphoreType.DMA((size - 1,)),
            pltpu.SemaphoreType.DMA,
        ],
        compiler_params=pltpu.CompilerParams(collective_id=collective_id, has_side_effects=True),
    )(blocks)


def mix_kernel(
    partial_ref,
    residual_ref,
    meta_ref,
    rows_ref,
    all_meta_ref,
    mixed_ref,
    half_slot,
    half_sum,
    part_slot,
    half_send,
    half_recv,
    part_send,
    part_recv,
    row_send,
    row_recv,
    col_send,
    col_recv,
    side_send,
    side_recv,
    meta_send,
    meta_recv,
):
    r, d, t = lax.axis_index("role"), lax.axis_index("dp"), lax.axis_index("tensor")
    dps, tensors = lax.axis_size("dp"), lax.axis_size("tensor")
    group = mixed_ref.shape[0]
    half = tensors * group
    other = 1 - r
    greet(("role", "tensor", "dp"))

    def rows(role, first, count=group):
        return pl.ds(pl.multiple_of(role * half + first * group, group), count)

    halves = remote(
        partial_ref.at[rows(other, 0, half)], half_slot, half_send, half_recv, "role", other
    )
    halves.start()
    all_meta_ref[rows(r, t)] = meta_ref[...]
    metas = []
    for j in range(1, tensors):
        copy = remote(
            meta_ref,
            all_meta_ref.at[rows(r, t)],
            meta_send.at[j],
            meta_recv.at[j],
            "tensor",
            peer_of("tensor", j),
        )
        copy.start()
        metas.append(copy)
    halves.wait()
    half_sum[...] = (
        partial_ref[rows(r, 0, half)].astype(jnp.float32) + half_slot[...].astype(jnp.float32)
    ).astype(jnp.bfloat16)
    parts = []
    for j in range(1, tensors):
        peer = peer_of("tensor", j)
        copy = remote(
            half_sum.at[pl.ds(pl.multiple_of(peer * group, group), group)],
            part_slot.at[j - 1],
            part_send.at[j - 1],
            part_recv.at[j - 1],
            "tensor",
            peer,
        )
        copy.start()
        parts.append(copy)
    for copy in metas:
        copy.wait()
    side_meta = remote(
        all_meta_ref.at[rows(r, 0, half)],
        all_meta_ref.at[rows(r, 0, half)],
        meta_send.at[0],
        meta_recv.at[0],
        "role",
        other,
    )
    side_meta.start()
    total = residual_ref[...].astype(jnp.float32) + half_sum[
        pl.ds(pl.multiple_of(t * group, group), group)
    ].astype(jnp.float32)
    for j in range(1, tensors):
        parts[j - 1].wait()
        total = total + part_slot[j - 1].astype(jnp.float32)
    mixed = total.astype(jnp.bfloat16)
    mixed_ref[...] = mixed
    rows_ref[d, rows(r, t)] = mixed
    along, across, sides = [], {}, []
    for j in range(1, tensors):
        copy = remote(
            mixed_ref,
            rows_ref.at[d, rows(r, t)],
            row_send.at[j - 1],
            row_recv.at[j - 1],
            "tensor",
            peer_of("tensor", j),
        )
        copy.start()
        along.append(copy)
    for j in range(tensors):
        if j > 0:
            along[j - 1].wait()
        block = rows_ref.at[d, rows(r, source_of("tensor", j))]
        for k in range(1, dps):
            copy = remote(
                block, block, col_send.at[k - 1, j], col_recv.at[k - 1, j], "dp", peer_of("dp", k)
            )
            copy.start()
            across[k, j] = copy
    for k in range(dps):
        for j in range(tensors if k > 0 else 0):
            across[k, j].wait()
        block = rows_ref.at[source_of("dp", k), rows(r, 0, half)]
        copy = remote(block, block, side_send.at[k], side_recv.at[k], "role", other)
        copy.start()
        sides.append(copy)
    side_meta.wait()
    for copy in sides:
        copy.wait()


def mix_rows(partial, residual, meta):
    dps, tensors = lax.axis_size("dp"), lax.axis_size("tensor")
    group, width = residual.shape
    tokens = partial.shape[0]
    half = tokens // 2
    vmem = pl.BlockSpec(memory_space=pltpu.VMEM)
    dma = pltpu.SemaphoreType.DMA
    return pl.pallas_call(
        mix_kernel,
        out_shape=[
            jax.ShapeDtypeStruct((dps, tokens, width), jnp.bfloat16),
            jax.ShapeDtypeStruct((tokens, meta.shape[1]), jnp.float32),
            jax.ShapeDtypeStruct((group, width), jnp.bfloat16),
        ],
        in_specs=[vmem] * 3,
        out_specs=[vmem] * 3,
        scratch_shapes=[
            pltpu.VMEM((half, width), jnp.bfloat16),
            pltpu.VMEM((half, width), jnp.bfloat16),
            pltpu.VMEM((tensors - 1, group, width), jnp.bfloat16),
            dma,
            dma,
            dma((tensors - 1,)),
            dma((tensors - 1,)),
            dma((tensors - 1,)),
            dma((tensors - 1,)),
            dma((dps - 1, tensors)),
            dma((dps - 1, tensors)),
            dma((dps,)),
            dma((dps,)),
            dma((tensors,)),
            dma((tensors,)),
        ],
        compiler_params=pltpu.CompilerParams(
            collective_id=2, has_side_effects=True, vmem_limit_bytes=VMEM_BYTES
        ),
    )(partial, residual, meta)


def reduce_kernel(
    partial_ref,
    mixed_ref,
    out_ref,
    side_slot,
    side_sum,
    col_slot,
    half_sum,
    part_slot,
    side_send,
    side_recv,
    col_send,
    col_recv,
    part_send,
    part_recv,
):
    r, t = lax.axis_index("role"), lax.axis_index("tensor")
    dps, tensors = lax.axis_size("dp"), lax.axis_size("tensor")
    group = mixed_ref.shape[0]
    half = tensors * group
    other = 1 - r
    greet(("role", "tensor", "dp"))
    mine = pl.ds(pl.multiple_of(r * half, group), half)
    theirs = pl.ds(pl.multiple_of(other * half, group), half)
    order = [*range(1, dps), 0]
    sides, cols = {}, []
    for k in order:
        copy = remote(
            partial_ref.at[peer_of("dp", k), theirs],
            side_slot.at[k],
            side_send.at[k],
            side_recv.at[k],
            "role",
            other,
        )
        copy.start()
        sides[k] = copy
    for k in order:
        sides[k].wait()
        total = partial_ref[peer_of("dp", k), mine].astype(jnp.float32) + side_slot[k].astype(
            jnp.float32
        )
        if k > 0:
            side_sum[k - 1] = total.astype(jnp.bfloat16)
            copy = remote(
                side_sum.at[k - 1],
                col_slot.at[k - 1],
                col_send.at[k - 1],
                col_recv.at[k - 1],
                "dp",
                peer_of("dp", k),
            )
            copy.start()
            cols.append(copy)
        else:
            half_sum[...] = total
    for k in range(1, dps):
        cols[k - 1].wait()
        half_sum[...] += col_slot[k - 1].astype(jnp.float32)
    side_sum[dps - 1] = half_sum[...].astype(jnp.bfloat16)
    parts = []
    for j in range(1, tensors):
        peer = peer_of("tensor", j)
        copy = remote(
            side_sum.at[dps - 1, pl.ds(pl.multiple_of(peer * group, group), group)],
            part_slot.at[j - 1],
            part_send.at[j - 1],
            part_recv.at[j - 1],
            "tensor",
            peer,
        )
        copy.start()
        parts.append(copy)
    total = (
        mixed_ref[...].astype(jnp.float32) + half_sum[pl.ds(pl.multiple_of(t * group, group), group)]
    )
    for j in range(1, tensors):
        parts[j - 1].wait()
        total = total + part_slot[j - 1].astype(jnp.float32)
    out_ref[...] = total.astype(jnp.bfloat16)


def reduce_rows(partial, mixed_in):
    dps, tensors = lax.axis_size("dp"), lax.axis_size("tensor")
    group, width = mixed_in.shape
    half = tensors * group
    vmem = pl.BlockSpec(memory_space=pltpu.VMEM)
    dma = pltpu.SemaphoreType.DMA
    return pl.pallas_call(
        reduce_kernel,
        out_shape=jax.ShapeDtypeStruct((group, width), jnp.bfloat16),
        in_specs=[vmem] * 2,
        out_specs=vmem,
        scratch_shapes=[
            pltpu.VMEM((dps, half, width), jnp.bfloat16),
            pltpu.VMEM((dps, half, width), jnp.bfloat16),
            pltpu.VMEM((dps - 1, half, width), jnp.bfloat16),
            pltpu.VMEM((half, width), jnp.float32),
            pltpu.VMEM((tensors - 1, group, width), jnp.bfloat16),
            dma((dps,)),
            dma((dps,)),
            dma((dps - 1,)),
            dma((dps - 1,)),
            dma((tensors - 1,)),
            dma((tensors - 1,)),
        ],
        compiler_params=pltpu.CompilerParams(
            collective_id=3, has_side_effects=True, vmem_limit_bytes=VMEM_BYTES
        ),
    )(partial, mixed_in)


def hidden_kernel(
    rows_ref,
    gain_ref,
    meta_ref,
    gates_ref,
    gate_w_ref,
    up_w_ref,
    left_ref,
    hidden_ref,
    coef_ref,
    normed,
    gate_acc,
    up_acc,
):
    step = pl.program_id(1)
    dps, tokens, width = rows_ref.shape

    @pl.when((pl.program_id(0) == 0) & (step == 0))
    def _():
        square = jnp.zeros((tokens, 1), jnp.float32)
        for k in range(dps):
            wide = rows_ref[k].astype(jnp.float32)
            square = square + jnp.sum(wide * wide, axis=1, keepdims=True)
        scale = lax.rsqrt(square / (dps * width) + NORM_EPS)
        for k in range(dps):
            wide = rows_ref[k].astype(jnp.float32)
            normed[k] = (wide * scale * gain_ref[k].astype(jnp.float32)).astype(jnp.bfloat16)

    @pl.when(step == 0)
    def _():
        gate_acc[...] = jnp.zeros_like(gate_acc)
        up_acc[...] = jnp.zeros_like(up_acc)

    block = normed[step]
    gate_acc[...] += jnp.dot(block, gate_w_ref[0], preferred_element_type=jnp.float32)
    up_acc[...] += jnp.dot(block, up_w_ref[0], preferred_element_type=jnp.float32)

    @pl.when(step == dps - 1)
    def _():
        gate = gate_acc[...]
        value = gate / (1.0 + jnp.exp(-gate)) * up_acc[...]
        value = jnp.where(gates_ref[0] > 0.0, value * gates_ref[0], 0.0)
        hidden = value.astype(jnp.bfloat16)
        hidden_ref[0] = hidden
        owner = meta_ref[:, EXPERTS : EXPERTS + 1]
        for tenant in range(TEN):
            coef = jnp.dot(hidden, left_ref[tenant, 0], preferred_element_type=jnp.float32)
            coef = jnp.where(owner == tenant, -coef, 0.0)
            coef_ref[tenant, 0] = coef.astype(jnp.bfloat16)


def hidden_rows(rows, gain, meta, gates, gate_w, up_w, left):
    dps, tokens, width = rows.shape
    experts, _, units = gate_w.shape
    rank = left.shape[-1]
    return pl.pallas_call(
        hidden_kernel,
        grid=(experts, dps),
        out_shape=[
            jax.ShapeDtypeStruct((experts, tokens, units), jnp.bfloat16),
            jax.ShapeDtypeStruct((TEN, experts, tokens, rank), jnp.bfloat16),
        ],
        in_specs=[
            pl.BlockSpec((dps, tokens, width), lambda e, k: (0, 0, 0)),
            pl.BlockSpec((dps, 1, width), lambda e, k: (0, 0, 0)),
            pl.BlockSpec(meta.shape, lambda e, k: (0, 0)),
            pl.BlockSpec((1, tokens, 1), lambda e, k: (e, 0, 0)),
            pl.BlockSpec((1, width, units), lambda e, k: (e, k, 0)),
            pl.BlockSpec((1, width, units), lambda e, k: (e, k, 0)),
            pl.BlockSpec((TEN, 1, units, rank), lambda e, k: (0, e, 0, 0)),
        ],
        out_specs=[
            pl.BlockSpec((1, tokens, units), lambda e, k: (e, 0, 0)),
            pl.BlockSpec((TEN, 1, tokens, rank), lambda e, k: (0, e, 0, 0)),
        ],
        scratch_shapes=[
            pltpu.VMEM((dps, tokens, width), jnp.bfloat16),
            pltpu.VMEM((tokens, units), jnp.float32),
            pltpu.VMEM((tokens, units), jnp.float32),
        ],
        compiler_params=pltpu.CompilerParams(vmem_limit_bytes=VMEM_BYTES),
    )(rows, gain, meta, gates, gate_w, up_w, left)


def down_kernel(hidden_ref, coef_ref, down_ref, right_ref, out_ref):
    experts = hidden_ref.shape[0]
    total = None
    for e in range(experts):
        term = jnp.dot(hidden_ref[e], down_ref[e], preferred_element_type=jnp.float32)
        total = term if total is None else total + term
        for tenant in range(TEN):
            total = total + jnp.dot(
                coef_ref[tenant, e], right_ref[tenant, e], preferred_element_type=jnp.float32
            )
    out_ref[...] = total.astype(jnp.bfloat16)


def down_rows(hidden, coef, down, right, dps):
    experts, tokens, units = hidden.shape
    model = down.shape[2]
    rank = coef.shape[-1]
    width = model // dps
    direct = width % 256 == 0
    block = 256
    per = width // block
    shape = (dps, tokens, width) if direct else (tokens, model)
    if direct:
        out_spec = pl.BlockSpec((None, tokens, block), lambda c: (c // per, 0, c % per))
    else:
        out_spec = pl.BlockSpec((tokens, block), lambda c: (0, c))
    out = pl.pallas_call(
        down_kernel,
        grid=(model // block,),
        out_shape=jax.ShapeDtypeStruct(shape, jnp.bfloat16),
        in_specs=[
            pl.BlockSpec((experts, tokens, units), lambda c: (0, 0, 0)),
            pl.BlockSpec((TEN, experts, tokens, rank), lambda c: (0, 0, 0, 0)),
            pl.BlockSpec((experts, units, block), lambda c: (0, 0, c)),
            pl.BlockSpec(
                (TEN, experts, rank, block), lambda c: (0, 0, 0, c)
            ),
        ],
        out_specs=out_spec,
        compiler_params=pltpu.CompilerParams(vmem_limit_bytes=VMEM_BYTES),
    )(hidden, coef, down, right)
    if not direct:
        out = jnp.transpose(out.reshape(tokens, dps, width), (1, 0, 2))
    return out


def local(
    queries,
    latent_cache,
    new_latent,
    cache_lengths,
    value_proj,
    out_proj,
    residual,
    norm_gain,
    routes,
    gate_values,
    tenant_ids,
    expert_gate_weight,
    expert_up_weight,
    expert_down_weight,
    left_delta_factor,
    factor_right,
):
    seq_count, context, width = latent_cache.shape
    local_heads = queries.shape[1]
    paired = queries.reshape(seq_count, 2, local_heads, width)
    scores = (
        jnp.einsum("sqhd,spd->sqhp", paired, latent_cache, preferred_element_type=jnp.float32)
        * SCORE_SCALE
    )
    present = jnp.arange(context, dtype=jnp.int32)[None, :] < cache_lengths[:, None]
    scores = jnp.where(present[:, None, None, :], scores, MASKED)
    fresh_keys = new_latent.reshape(seq_count, 2, width)
    fresh = (
        jnp.einsum("sqhd,skd->sqhk", paired, fresh_keys, preferred_element_type=jnp.float32)
        * SCORE_SCALE
    )
    causal = jnp.arange(2)[:, None] >= jnp.arange(2)[None, :]
    fresh = jnp.where(causal[None, :, None, :], fresh, MASKED)
    top = jnp.maximum(jnp.max(scores, axis=3), jnp.max(fresh, axis=3))[..., None]
    weights = jnp.exp(scores - top)
    fresh_weights = jnp.exp(fresh - top)
    total = jnp.sum(weights, axis=3) + jnp.sum(fresh_weights, axis=3)
    summed = jnp.einsum(
        "sqhp,spd->sqhd",
        weights.astype(jnp.bfloat16),
        latent_cache[:, :, :LAT],
        preferred_element_type=jnp.float32,
    )
    summed = summed + jnp.einsum(
        "sqhk,skd->sqhd",
        fresh_weights.astype(jnp.bfloat16),
        fresh_keys[:, :, :LAT],
        preferred_element_type=jnp.float32,
    )
    attended = (
        (summed / total[..., None]).astype(jnp.bfloat16).reshape(seq_count * 2, local_heads, LAT)
    )
    dps, tensors = lax.axis_size("dp"), lax.axis_size("tensor")
    own_heads = local_heads // tensors
    blocks = jnp.transpose(
        attended.reshape(seq_count * 2, tensors, own_heads, LAT), (1, 0, 2, 3)
    ).reshape(tensors, seq_count * 2 * own_heads, LAT)
    by_head = exchange(blocks, "tensor", False, 0).reshape(
        tensors * seq_count * 2, own_heads, LAT
    )
    head_values = jnp.einsum(
        "thl,hlv->thv", by_head, value_proj, preferred_element_type=jnp.float32
    ).astype(jnp.bfloat16)
    head_values = head_values.reshape(by_head.shape[0], -1)
    all_values = exchange(head_values, "dp", True, 1).reshape(-1, head_values.shape[1])
    partial = jnp.dot(all_values, out_proj, preferred_element_type=jnp.float32).astype(jnp.bfloat16)
    chosen = routes[:, :, None] == jnp.arange(EXPERTS, dtype=jnp.int32)[None, None, :]
    gate_of = jnp.sum(jnp.where(chosen, gate_values[:, :, None], 0.0), axis=1)
    meta = jnp.concatenate([gate_of, tenant_ids[:, None].astype(jnp.float32)], axis=1)
    meta = jnp.pad(meta, ((0, 0), (0, 128 - meta.shape[1])))
    rows, all_meta, mixed_in = mix_rows(partial, residual, meta)
    local_experts = EXPERTS // dps
    expert_start = lax.axis_index("dp") * local_experts
    own_gates = lax.dynamic_slice_in_dim(all_meta, expert_start, local_experts, 1).T[:, :, None]
    hidden, coef = hidden_rows(
        rows,
        norm_gain.reshape(dps, 1, -1),
        all_meta,
        own_gates,
        expert_gate_weight,
        expert_up_weight,
        left_delta_factor,
    )
    experts_part = down_rows(hidden, coef, expert_down_weight, factor_right, dps)
    return reduce_rows(experts_part, mixed_in)


def solution(mesh):
    placed = (
        P(("dp", "tensor"), "role", None),
        P(("dp", "tensor"), None, None),
        P(("dp", "tensor"), None),
        P(("dp", "tensor")),
        P(("role", "tensor"), None, None),
        P(("role", "tensor"), "dp"),
        P(("role", "tensor"), "dp"),
        P(),
        P(("role", "tensor"), None),
        P(("role", "tensor"), None),
        P(("role", "tensor")),
        P("dp", None, ("role", "tensor")),
        P("dp", None, ("role", "tensor")),
        P("dp", ("role", "tensor"), None),
        P(None, "dp", ("role", "tensor"), None),
        P(None, "dp", None, None),
    )
    return jax.shard_map(
        local, mesh=mesh, in_specs=placed, out_specs=P(("role", "tensor"), "dp"), check_vma=False
    )
```

```python
import functools
import jax
import jax.numpy as jnp
from jax import lax
from jax.experimental import pallas as pl
from jax.experimental.pallas import tpu as pltpu
from jax.sharding import PartitionSpec as P

LAT = 512
EXPERTS = 16
TEN = 3


SCORE_SCALE = 0.07216878364870323
NORM_EPS = 1e-06
MASKED = -1e30


MESH = pl.DeviceIdType.MESH
VMEM_BYTES = 56 * 1024 * 1024


def peer_of(axis, offset):
    size = lax.axis_size(axis)
    return lax.rem(lax.axis_index(axis) + offset, size)


def source_of(axis, offset):
    size = lax.axis_size(axis)
    return lax.rem(lax.axis_index(axis) + size - offset, size)


def greet(axes):
    barrier = pltpu.get_barrier_semaphore()
    count = 0
    for axis in axes:
        for offset in range(1, lax.axis_size(axis)):
            pl.semaphore_signal(
                barrier, inc=1, device_id={axis: peer_of(axis, offset)}, device_id_type=MESH
            )
            count += 1
    pl.semaphore_wait(barrier, count)


def remote(source, target, send, recv, axis, peer):
    return pltpu.make_async_remote_copy(
        src_ref=source,
        dst_ref=target,
        send_sem=send,
        recv_sem=recv,
        device_id={axis: peer},
        device_id_type=MESH,
    )


def attend_kernel(
    lengths_ref, query_ref, cache_ref, fresh_ref, out_ref, keys_ref, stage, load, send, recv
):
    heads, width = query_ref.shape[1:]
    tensors, seqs, _, own_heads, _ = out_ref.shape
    loads = []
    for s in range(seqs):
        copy = pltpu.make_async_copy(cache_ref.at[s], keys_ref.at[s], load.at[s])
        copy.start()
        loads.append(copy)
    greet(("tensor",))
    me = lax.axis_index("tensor")
    copies = []
    for s in range(seqs):
        query = query_ref[2 * s : 2 * s + 2].reshape(2 * heads, width)
        loads[s].wait()
        scores = jnp.dot(query, keys_ref[s], preferred_element_type=jnp.float32) * SCORE_SCALE
        place = lax.broadcasted_iota(jnp.int32, scores.shape, 1)
        scores = jnp.where(place < lengths_ref[s], scores, MASKED)
        wide = query.astype(jnp.float32)
        keys = [fresh_ref[s, i : i + 1].astype(jnp.float32) for i in range(2)]
        fresh = [jnp.sum(wide * key, axis=1, keepdims=True) * SCORE_SCALE for key in keys]
        later = lax.broadcasted_iota(jnp.int32, fresh[1].shape, 0) >= heads
        fresh[1] = jnp.where(later, fresh[1], MASKED)
        top = jnp.maximum(
            jnp.max(scores, axis=1, keepdims=True), jnp.maximum(fresh[0], fresh[1])
        )
        weights = jnp.exp(scores - top)
        fresh = [jnp.exp(score - top) for score in fresh]
        total = jnp.sum(weights, axis=1, keepdims=True) + fresh[0] + fresh[1]
        summed = lax.dot_general(
            weights.astype(jnp.bfloat16),
            keys_ref[s, :LAT],
            (((1,), (1,)), ((), ())),
            preferred_element_type=jnp.float32,
        )
        for weight, key in zip(fresh, keys):
            summed = summed + weight.astype(jnp.bfloat16).astype(jnp.float32) * key[:, :LAT]
        attended = (summed / total).astype(jnp.bfloat16)
        for step in range(2):
            for part in range(tensors):
                first = step * heads + part * own_heads
                stage[part, s, step] = attended[first : first + own_heads]
        for j in range(1, tensors):
            peer = peer_of("tensor", j)
            copy = remote(
                stage.at[peer, s],
                out_ref.at[me, s],
                send.at[s, j - 1],
                recv.at[s, j - 1],
                "tensor",
                peer,
            )
            copy.start()
            copies.append(copy)
        out_ref[me, s] = stage[me, s]
    for copy in copies:
        copy.wait()


def attend(queries, latent_cache, new_latent, cache_lengths, tensors):
    heads, width = queries.shape[1:]
    seqs, context, _ = latent_cache.shape
    own_heads = heads // tensors
    vmem = pl.BlockSpec(memory_space=pltpu.VMEM)
    shape = (tensors, seqs, 2, own_heads, LAT)
    return pl.pallas_call(
        attend_kernel,
        out_shape=jax.ShapeDtypeStruct(shape, jnp.bfloat16),
        in_specs=[
            pl.BlockSpec(memory_space=pltpu.SMEM),
            vmem,
            pl.BlockSpec(memory_space=pl.ANY),
            vmem,
        ],
        out_specs=vmem,
        scratch_shapes=[
            pltpu.VMEM((seqs, width, context), jnp.bfloat16),
            pltpu.VMEM(shape, jnp.bfloat16),
            pltpu.SemaphoreType.DMA((seqs,)),
            pltpu.SemaphoreType.DMA((seqs, tensors - 1)),
            pltpu.SemaphoreType.DMA((seqs, tensors - 1)),
        ],
        compiler_params=pltpu.CompilerParams(
            collective_id=0, has_side_effects=True, vmem_limit_bytes=VMEM_BYTES
        ),
    )(
        cache_lengths,
        queries,
        jnp.swapaxes(latent_cache, 1, 2),
        new_latent.reshape(seqs, 2, width),
    )


def exchange_kernel(axis, gather, block_ref, out_ref, send, recv, own_sem):
    size = lax.axis_size(axis)
    me = lax.axis_index(axis)
    own = pltpu.make_async_copy(
        block_ref if gather else block_ref.at[me], out_ref.at[me], own_sem
    )
    own.start()
    greet((axis,))
    copies = []
    for offset in range(1, size):
        peer = peer_of(axis, offset)
        copy = remote(
            block_ref if gather else block_ref.at[peer],
            out_ref.at[me],
            send.at[offset - 1],
            recv.at[offset - 1],
            axis,
            peer,
        )
        copy.start()
        copies.append(copy)
    own.wait()
    for copy in copies:
        copy.wait()


def exchange(blocks, axis, gather, collective_id):
    size = lax.axis_size(axis)
    shape = (size,) + blocks.shape if gather else blocks.shape
    return pl.pallas_call(
        functools.partial(exchange_kernel, axis, gather),
        out_shape=jax.ShapeDtypeStruct(shape, blocks.dtype),
        in_specs=[pl.BlockSpec(memory_space=pl.ANY)],
        out_specs=pl.BlockSpec(memory_space=pl.ANY),
        scratch_shapes=[
            pltpu.SemaphoreType.DMA((size - 1,)),
            pltpu.SemaphoreType.DMA((size - 1,)),
            pltpu.SemaphoreType.DMA,
        ],
        compiler_params=pltpu.CompilerParams(collective_id=collective_id, has_side_effects=True),
    )(blocks)


def mix_kernel(
    partial_ref,
    residual_ref,
    meta_ref,
    rows_ref,
    all_meta_ref,
    mixed_ref,
    half_slot,
    half_sum,
    part_slot,
    half_send,
    half_recv,
    part_send,
    part_recv,
    row_send,
    row_recv,
    col_send,
    col_recv,
    side_send,
    side_recv,
    meta_send,
    meta_recv,
):
    r, d, t = lax.axis_index("role"), lax.axis_index("dp"), lax.axis_index("tensor")
    dps, tensors = lax.axis_size("dp"), lax.axis_size("tensor")
    group = mixed_ref.shape[0]
    half = tensors * group
    other = 1 - r
    greet(("role", "tensor", "dp"))

    def rows(role, first, count=group):
        return pl.ds(pl.multiple_of(role * half + first * group, group), count)

    halves = remote(
        partial_ref.at[rows(other, 0, half)], half_slot, half_send, half_recv, "role", other
    )
    halves.start()
    all_meta_ref[rows(r, t)] = meta_ref[...]
    metas = []
    for j in range(1, tensors):
        copy = remote(
            meta_ref,
            all_meta_ref.at[rows(r, t)],
            meta_send.at[j],
            meta_recv.at[j],
            "tensor",
            peer_of("tensor", j),
        )
        copy.start()
        metas.append(copy)
    halves.wait()
    half_sum[...] = (
        partial_ref[rows(r, 0, half)].astype(jnp.float32) + half_slot[...].astype(jnp.float32)
    ).astype(jnp.bfloat16)
    parts = []
    for j in range(1, tensors):
        peer = peer_of("tensor", j)
        copy = remote(
            half_sum.at[pl.ds(pl.multiple_of(peer * group, group), group)],
            part_slot.at[j - 1],
            part_send.at[j - 1],
            part_recv.at[j - 1],
            "tensor",
            peer,
        )
        copy.start()
        parts.append(copy)
    for copy in metas:
        copy.wait()
    side_meta = remote(
        all_meta_ref.at[rows(r, 0, half)],
        all_meta_ref.at[rows(r, 0, half)],
        meta_send.at[0],
        meta_recv.at[0],
        "role",
        other,
    )
    side_meta.start()
    total = residual_ref[...].astype(jnp.float32) + half_sum[
        pl.ds(pl.multiple_of(t * group, group), group)
    ].astype(jnp.float32)
    for j in range(1, tensors):
        parts[j - 1].wait()
        total = total + part_slot[j - 1].astype(jnp.float32)
    mixed = total.astype(jnp.bfloat16)
    mixed_ref[...] = mixed
    rows_ref[d, rows(r, t)] = mixed
    along, across, sides = [], {}, []
    for j in range(1, tensors):
        copy = remote(
            mixed_ref,
            rows_ref.at[d, rows(r, t)],
            row_send.at[j - 1],
            row_recv.at[j - 1],
            "tensor",
            peer_of("tensor", j),
        )
        copy.start()
        along.append(copy)
    for j in range(tensors):
        if j > 0:
            along[j - 1].wait()
        block = rows_ref.at[d, rows(r, source_of("tensor", j))]
        for k in range(1, dps):
            copy = remote(
                block, block, col_send.at[k - 1, j], col_recv.at[k - 1, j], "dp", peer_of("dp", k)
            )
            copy.start()
            across[k, j] = copy
    for k in range(dps):
        for j in range(tensors if k > 0 else 0):
            across[k, j].wait()
        block = rows_ref.at[source_of("dp", k), rows(r, 0, half)]
        copy = remote(block, block, side_send.at[k], side_recv.at[k], "role", other)
        copy.start()
        sides.append(copy)
    side_meta.wait()
    for copy in sides:
        copy.wait()


def mix_rows(partial, residual, meta):
    dps, tensors = lax.axis_size("dp"), lax.axis_size("tensor")
    group, width = residual.shape
    tokens = partial.shape[0]
    half = tokens // 2
    vmem = pl.BlockSpec(memory_space=pltpu.VMEM)
    dma = pltpu.SemaphoreType.DMA
    return pl.pallas_call(
        mix_kernel,
        out_shape=[
            jax.ShapeDtypeStruct((dps, tokens, width), jnp.bfloat16),
            jax.ShapeDtypeStruct((tokens, meta.shape[1]), jnp.float32),
            jax.ShapeDtypeStruct((group, width), jnp.bfloat16),
        ],
        in_specs=[vmem] * 3,
        out_specs=[vmem] * 3,
        scratch_shapes=[
            pltpu.VMEM((half, width), jnp.bfloat16),
            pltpu.VMEM((half, width), jnp.bfloat16),
            pltpu.VMEM((tensors - 1, group, width), jnp.bfloat16),
            dma,
            dma,
            dma((tensors - 1,)),
            dma((tensors - 1,)),
            dma((tensors - 1,)),
            dma((tensors - 1,)),
            dma((dps - 1, tensors)),
            dma((dps - 1, tensors)),
            dma((dps,)),
            dma((dps,)),
            dma((tensors,)),
            dma((tensors,)),
        ],
        compiler_params=pltpu.CompilerParams(
            collective_id=2, has_side_effects=True, vmem_limit_bytes=VMEM_BYTES
        ),
    )(partial, residual, meta)


def reduce_kernel(
    partial_ref,
    mixed_ref,
    out_ref,
    side_slot,
    side_sum,
    col_slot,
    half_sum,
    part_slot,
    side_send,
    side_recv,
    col_send,
    col_recv,
    part_send,
    part_recv,
):
    r, t = lax.axis_index("role"), lax.axis_index("tensor")
    dps, tensors = lax.axis_size("dp"), lax.axis_size("tensor")
    group = mixed_ref.shape[0]
    half = tensors * group
    other = 1 - r
    greet(("role", "tensor", "dp"))
    mine = pl.ds(pl.multiple_of(r * half, group), half)
    theirs = pl.ds(pl.multiple_of(other * half, group), half)
    order = [*range(1, dps), 0]
    sides, cols = {}, []
    for k in order:
        copy = remote(
            partial_ref.at[peer_of("dp", k), theirs],
            side_slot.at[k],
            side_send.at[k],
            side_recv.at[k],
            "role",
            other,
        )
        copy.start()
        sides[k] = copy
    for k in order:
        sides[k].wait()
        total = partial_ref[peer_of("dp", k), mine].astype(jnp.float32) + side_slot[k].astype(
            jnp.float32
        )
        if k > 0:
            side_sum[k - 1] = total.astype(jnp.bfloat16)
            copy = remote(
                side_sum.at[k - 1],
                col_slot.at[k - 1],
                col_send.at[k - 1],
                col_recv.at[k - 1],
                "dp",
                peer_of("dp", k),
            )
            copy.start()
            cols.append(copy)
        else:
            half_sum[...] = total
    for k in range(1, dps):
        cols[k - 1].wait()
        half_sum[...] += col_slot[k - 1].astype(jnp.float32)
    side_sum[dps - 1] = half_sum[...].astype(jnp.bfloat16)
    parts = []
    for j in range(1, tensors):
        peer = peer_of("tensor", j)
        copy = remote(
            side_sum.at[dps - 1, pl.ds(pl.multiple_of(peer * group, group), group)],
            part_slot.at[j - 1],
            part_send.at[j - 1],
            part_recv.at[j - 1],
            "tensor",
            peer,
        )
        copy.start()
        parts.append(copy)
    total = (
        mixed_ref[...].astype(jnp.float32) + half_sum[pl.ds(pl.multiple_of(t * group, group), group)]
    )
    for j in range(1, tensors):
        parts[j - 1].wait()
        total = total + part_slot[j - 1].astype(jnp.float32)
    out_ref[...] = total.astype(jnp.bfloat16)


def reduce_rows(partial, mixed_in):
    dps, tensors = lax.axis_size("dp"), lax.axis_size("tensor")
    group, width = mixed_in.shape
    half = tensors * group
    vmem = pl.BlockSpec(memory_space=pltpu.VMEM)
    dma = pltpu.SemaphoreType.DMA
    return pl.pallas_call(
        reduce_kernel,
        out_shape=jax.ShapeDtypeStruct((group, width), jnp.bfloat16),
        in_specs=[vmem] * 2,
        out_specs=vmem,
        scratch_shapes=[
            pltpu.VMEM((dps, half, width), jnp.bfloat16),
            pltpu.VMEM((dps, half, width), jnp.bfloat16),
            pltpu.VMEM((dps - 1, half, width), jnp.bfloat16),
            pltpu.VMEM((half, width), jnp.float32),
            pltpu.VMEM((tensors - 1, group, width), jnp.bfloat16),
            dma((dps,)),
            dma((dps,)),
            dma((dps - 1,)),
            dma((dps - 1,)),
            dma((tensors - 1,)),
            dma((tensors - 1,)),
        ],
        compiler_params=pltpu.CompilerParams(
            collective_id=3, has_side_effects=True, vmem_limit_bytes=VMEM_BYTES
        ),
    )(partial, mixed_in)


def hidden_kernel(
    rows_ref,
    gain_ref,
    meta_ref,
    gate_w_ref,
    up_w_ref,
    left_ref,
    hidden_ref,
    coef_ref,
    normed,
    gate_acc,
    up_acc,
):
    step = pl.program_id(1)
    dps, tokens, width = rows_ref.shape

    @pl.when((pl.program_id(0) == 0) & (step == 0))
    def _():
        square = jnp.zeros((tokens, 1), jnp.float32)
        for k in range(dps):
            wide = rows_ref[k].astype(jnp.float32)
            square = square + jnp.sum(wide * wide, axis=1, keepdims=True)
        scale = lax.rsqrt(square / (dps * width) + NORM_EPS)
        for k in range(dps):
            wide = rows_ref[k].astype(jnp.float32)
            normed[k] = (wide * scale * gain_ref[k].astype(jnp.float32)).astype(jnp.bfloat16)

    @pl.when(step == 0)
    def _():
        gate_acc[...] = jnp.zeros_like(gate_acc)
        up_acc[...] = jnp.zeros_like(up_acc)

    block = normed[step]
    gate_acc[...] += jnp.dot(block, gate_w_ref[0], preferred_element_type=jnp.float32)
    up_acc[...] += jnp.dot(block, up_w_ref[0], preferred_element_type=jnp.float32)

    @pl.when(step == dps - 1)
    def _():
        gate = gate_acc[...]
        value = gate / (1.0 + jnp.exp(-gate)) * up_acc[...]
        label = lax.axis_index("dp") * pl.num_programs(0) + pl.program_id(0)
        lane = lax.broadcasted_iota(jnp.int32, meta_ref.shape, 1)
        own = jnp.sum(jnp.where(lane == label, meta_ref[...], 0.0), axis=1, keepdims=True)
        value = jnp.where(own > 0.0, value * own, 0.0)
        hidden = value.astype(jnp.bfloat16)
        hidden_ref[0] = hidden
        owner = meta_ref[:, EXPERTS : EXPERTS + 1]
        coef = jnp.dot(hidden, left_ref[0], preferred_element_type=jnp.float32)
        tenant = lax.broadcasted_iota(jnp.int32, coef.shape, 1) // (coef.shape[1] // TEN)
        coef = jnp.where(owner == tenant.astype(jnp.float32), -coef, 0.0)
        coef_ref[0] = coef.astype(jnp.bfloat16)


def hidden_rows(rows, gain, meta, gate_w, up_w, left):
    dps, tokens, width = rows.shape
    experts, _, units = gate_w.shape
    depth = left.shape[-1]
    return pl.pallas_call(
        hidden_kernel,
        grid=(experts, dps),
        out_shape=[
            jax.ShapeDtypeStruct((experts, tokens, units), jnp.bfloat16),
            jax.ShapeDtypeStruct((experts, tokens, depth), jnp.bfloat16),
        ],
        in_specs=[
            pl.BlockSpec((dps, tokens, width), lambda e, k: (0, 0, 0)),
            pl.BlockSpec((dps, 1, width), lambda e, k: (0, 0, 0)),
            pl.BlockSpec(meta.shape, lambda e, k: (0, 0)),
            pl.BlockSpec((1, width, units), lambda e, k: (e, k, 0)),
            pl.BlockSpec((1, width, units), lambda e, k: (e, k, 0)),
            pl.BlockSpec((1, units, depth), lambda e, k: (e, 0, 0)),
        ],
        out_specs=[
            pl.BlockSpec((1, tokens, units), lambda e, k: (e, 0, 0)),
            pl.BlockSpec((1, tokens, depth), lambda e, k: (e, 0, 0)),
        ],
        scratch_shapes=[
            pltpu.VMEM((dps, tokens, width), jnp.bfloat16),
            pltpu.VMEM((tokens, units), jnp.float32),
            pltpu.VMEM((tokens, units), jnp.float32),
        ],
        compiler_params=pltpu.CompilerParams(vmem_limit_bytes=VMEM_BYTES),
    )(rows, gain, meta, gate_w, up_w, left)


def down_kernel(hidden_ref, coef_ref, down_ref, right_ref, out_ref):
    experts = hidden_ref.shape[0]
    depth, block = coef_ref.shape[2], right_ref.shape[3]
    total = None
    for e in range(experts):
        term = jnp.dot(hidden_ref[e], down_ref[e], preferred_element_type=jnp.float32)
        total = term if total is None else total + term
        total = total + jnp.dot(
            coef_ref[e],
            right_ref[:, e].reshape(depth, block),
            preferred_element_type=jnp.float32,
        )
    out_ref[...] = total.astype(jnp.bfloat16)


def down_rows(hidden, coef, down, right, dps):
    experts, tokens, units = hidden.shape
    model = down.shape[2]
    depth = coef.shape[-1]
    rank = right.shape[2]
    width = model // dps
    direct = width % 896 == 0
    block = 896 if direct else 256
    per = max(width // block, 1)
    shape = (dps, tokens, width) if direct else (tokens, model)
    if direct:
        out_spec = pl.BlockSpec((None, tokens, block), lambda c: (c // per, 0, c % per))
    else:
        out_spec = pl.BlockSpec((tokens, block), lambda c: (0, c))
    out = pl.pallas_call(
        down_kernel,
        grid=(model // block,),
        out_shape=jax.ShapeDtypeStruct(shape, jnp.bfloat16),
        in_specs=[
            pl.BlockSpec((experts, tokens, units), lambda c: (0, 0, 0)),
            pl.BlockSpec((experts, tokens, depth), lambda c: (0, 0, 0)),
            pl.BlockSpec((experts, units, block), lambda c: (0, 0, c)),
            pl.BlockSpec(
                (TEN, experts, rank, block), lambda c: (0, 0, 0, c)
            ),
        ],
        out_specs=out_spec,
        compiler_params=pltpu.CompilerParams(vmem_limit_bytes=VMEM_BYTES),
    )(hidden, coef, down, right)
    if not direct:
        out = jnp.transpose(out.reshape(tokens, dps, width), (1, 0, 2))
    return out


def local(
    queries,
    latent_cache,
    new_latent,
    cache_lengths,
    value_proj,
    out_proj,
    residual,
    norm_gain,
    routes,
    gate_values,
    tenant_ids,
    expert_gate_weight,
    expert_up_weight,
    expert_down_weight,
    left_delta_factor,
    factor_right,
):
    seq_count = latent_cache.shape[0]
    dps, tensors = lax.axis_size("dp"), lax.axis_size("tensor")
    own_heads = queries.shape[1] // tensors
    by_head = attend(queries, latent_cache, new_latent, cache_lengths, tensors).reshape(
        tensors * seq_count * 2, own_heads, LAT
    )
    head_values = jnp.einsum(
        "thl,hlv->thv", by_head, value_proj, preferred_element_type=jnp.float32
    ).astype(jnp.bfloat16)
    head_values = head_values.reshape(by_head.shape[0], -1)
    all_values = exchange(head_values, "dp", True, 1).reshape(-1, head_values.shape[1])
    partial = jnp.dot(all_values, out_proj, preferred_element_type=jnp.float32).astype(jnp.bfloat16)
    chosen = routes[:, :, None] == jnp.arange(EXPERTS, dtype=jnp.int32)[None, None, :]
    gate_of = jnp.sum(jnp.where(chosen, gate_values[:, :, None], 0.0), axis=1)
    meta = jnp.concatenate([gate_of, tenant_ids[:, None].astype(jnp.float32)], axis=1)
    meta = jnp.pad(meta, ((0, 0), (0, 128 - meta.shape[1])))
    rows, all_meta, mixed_in = mix_rows(partial, residual, meta)
    left = jnp.transpose(left_delta_factor, (1, 2, 0, 3))
    left = left.reshape(left.shape[0], left.shape[1], -1)
    hidden, coef = hidden_rows(
        rows,
        norm_gain.reshape(dps, 1, -1),
        all_meta,
        expert_gate_weight,
        expert_up_weight,
        left,
    )
    experts_part = down_rows(hidden, coef, expert_down_weight, factor_right, dps)
    return reduce_rows(experts_part, mixed_in)


def solution(mesh):
    placed = (
        P(("dp", "tensor"), "role", None),
        P(("dp", "tensor"), None, None),
        P(("dp", "tensor"), None),
        P(("dp", "tensor")),
        P(("role", "tensor"), None, None),
        P(("role", "tensor"), "dp"),
        P(("role", "tensor"), "dp"),
        P(),
        P(("role", "tensor"), None),
        P(("role", "tensor"), None),
        P(("role", "tensor")),
        P("dp", None, ("role", "tensor")),
        P("dp", None, ("role", "tensor")),
        P("dp", ("role", "tensor"), None),
        P(None, "dp", ("role", "tensor"), None),
        P(None, "dp", None, None),
    )
    return jax.shard_map(
        local, mesh=mesh, in_specs=placed, out_specs=P(("role", "tensor"), "dp"), check_vma=False
    )
```
